32 devices in a mesh: row: 4 (over y, core), col: 8 (over z, x).
Axes of the slice: x: 2, y: 2, z: 4, core: 2. Of those that a mesh axis runs over, the one named last changes fastest.
Arguments:
- transition: bfloat16 [32768, 32768], P('row', 'col'), may hold values from 1.5258789e-06 to 0.0024414062, as said below
- emission: bfloat16 [96, 32768], P(None, 'col'), may hold values from 0.0099487305 to 1
- token_ids: int32 [2, 192], replicated, may hold values from 0 to 95
- forward: bfloat16 [2, 192, 32768], P(None, 'col', 'row'), may hold values from 3.0517578e-06 to 0.0008239746, as said below
- backward_last: float32 [192, 32768], P('row', 'col'), may hold values from 0.1 to 10
Outputs:
- backward: float32 [2, 192, 32768], P(None, 'col', 'row')
- counts: float32 [32768, 1024], P('row', 'col')
The draws below stay inside these ranges and needn't reach their ends.
Inputs may be any that keep to these rules, and one draw needn't show every extreme that they name: Positive transition weights. Positive forward weights.
All inputs are finite; a program needn't handle non-finite values.
Results may differ from the reference program's by a relative error of at most 0.00048.
Values may be sent and summed in bfloat16 or wider, within the bound.
A program may use at most 192 MiB of HBM per device.

```python
import math
import jax
import jax.numpy as jnp
from jax import lax

H = 32768
N = 192
DW = 128
U = 96
N_COL = 8


def draw_transition(key, part):
    base_key, pair_key, factor_key = jax.random.split(key, 3)
    pairing = jax.random.permutation(pair_key, 32)
    source_block = jnp.arange(H) * 16 // H
    dest_block = pairing[jnp.arange(H) * 32 // H] % 16
    boost = jnp.where(source_block[:, None] == dest_block[None, :], 4.0, 1.0)
    row_factor = jnp.exp(jax.random.uniform(factor_key, (H,), jnp.float32, math.log(0.125), math.log(8.0)))
    base = jnp.exp(jax.random.uniform(base_key, (H, H), jnp.float32, math.log(0.4), math.log(2.5)))
    return (base * row_factor[:, None] * boost / H).astype(jnp.bfloat16)


def draw_forward(key, part):
    states = jnp.arange(H).astype(jnp.float32) / H
    base = jnp.exp(jax.random.uniform(key, (2, N, H), jnp.float32, math.log(0.3), math.log(3.0)))
    ramp = 1.0 + 2.0 * states
    return (base * ramp[None, None, :] / H).astype(jnp.bfloat16)


def touch_ends(entries, own_key, smallest, top_value):
    longest = entries.shape.index(max(entries.shape))
    spots = []
    for shift in (0, 1):
        where = [jax.random.randint(jax.random.fold_in(own_key, axis), (), 0, length) for axis, length in enumerate(entries.shape)]
        where[longest] = (where[longest] + shift) % entries.shape[longest]
        spots.append(tuple(where))
    return entries.at[spots[0]].set(smallest).at[spots[1]].set(top_value)


def level_of(own_key, shape, cuts, low, largest):
    def one(axis_at, parts):
        heights = jax.random.uniform(jax.random.fold_in(jax.random.fold_in(own_key, 6), axis_at), (parts,), jnp.float32, low / len(cuts), largest / len(cuts))
        return jnp.repeat(jnp.exp(heights), shape[axis_at] // parts).reshape((-1,) + (1,) * (len(shape) - axis_at - 1))

    factor_of = one(*cuts[0])
    for cut in cuts[1:]:
        factor_of = factor_of * one(*cut)
    return factor_of


def setup_inputs(seed: int = 0) -> dict:
    key_list = jax.random.split(jax.random.key(seed), 6)
    transition = draw_transition(jax.random.fold_in(key_list[5], 71), 0)
    emission = jnp.clip(jnp.exp(math.log(1.0) - 4.61031033 * jax.random.uniform(key_list[1], (U, H), jnp.float32) ** level_of(key_list[1], (U, H), ((1, 8),), -0.2, 0.2)), 0.0099487305, 1.0).astype(jnp.bfloat16)
    token_ids = touch_ends(jax.random.randint(key_list[2], (2, N), 0, U), jax.random.fold_in(key_list[2], 1), 0, U - 1).astype(jnp.int32)
    forward = draw_forward(jax.random.fold_in(key_list[5], 71), 0)
    backward_last = jnp.clip(jnp.exp(math.log(10.0) - 4.6051702 * jax.random.uniform(key_list[4], (N, H), jnp.float32) ** level_of(key_list[4], (N, H), ((0, 4), (1, 8)), -0.2, 0.2)), 0.1, 10.0)
    return {"transition": transition, "emission": emission, "token_ids": token_ids, "forward": forward, "backward_last": backward_last}


def reference(transition, emission, token_ids, forward, backward_last):
    block_dst = H // N_COL
    window = transition.reshape(H, N_COL, block_dst)[:, :, :DW].reshape(H, N_COL * DW)
    totals = jnp.zeros((H, N_COL * DW), jnp.float32)
    backward_next = backward_last
    results = [None, None]
    for step in (1, 0):
        emitted = jnp.take(emission, token_ids[step], axis=0).astype(jnp.float32)
        weighted_back = (emitted * backward_next).astype(jnp.bfloat16)
        summed = lax.dot_general(weighted_back, transition, (((1,), (1,)), ((), ())), preferred_element_type=jnp.float32)
        alpha = forward[step].astype(jnp.float32)
        normal = jnp.sum(alpha * summed, axis=1)
        results[step] = summed / normal[:, None]
        scaled = (alpha / normal[:, None]).astype(jnp.bfloat16)
        picked = weighted_back.reshape(N, N_COL, block_dst)[:, :, :DW].reshape(N, N_COL * DW)
        totals = totals + jnp.dot(scaled.T, picked, preferred_element_type=jnp.float32)
        backward_next = results[step]
    counts = window.astype(jnp.float32) * totals * (H * H / N)
    return jnp.stack(results), counts
```

```python
import jax
import jax.numpy as jnp
from jax import lax
from jax.sharding import PartitionSpec as P

H = 32768
N = 192
DW = 128
CHUNKS = 2


def reduce_scatter(partial, scale, col_count, col_index, local_seqs):
    half = col_count // 2
    width = partial.shape[1]
    scaled = (partial * scale).reshape(half, 2, local_seqs, width)
    side = col_index % 2
    away = lax.dynamic_index_in_dim(scaled, 1 - side, 1, keepdims=False).astype(jnp.float16)
    got = lax.ppermute(away, "col", [(c, c ^ 1) for c in range(col_count)])
    pair = lax.dynamic_index_in_dim(scaled, side, 1, keepdims=False) + got.astype(jnp.float32)
    here = col_index // 2
    total = lax.dynamic_index_in_dim(pair, here, 0, keepdims=False)
    packed = pair.astype(jnp.float16)
    for k in range(1, half):
        piece = lax.dynamic_index_in_dim(packed, (here + k) % half, 0, keepdims=False)
        got = lax.ppermute(piece, "col", [(c, (c + 2 * k) % col_count) for c in range(col_count)])
        total = total + got.astype(jnp.float32)
    return total


def on_device(transition, emission, token_ids, forward, backward_last):
    row_count = lax.axis_size("row")
    col_count = lax.axis_size("col")
    row_index = lax.axis_index("row")
    col_index = lax.axis_index("col")
    ratio = col_count // row_count
    local_seqs = forward.shape[1]
    row_seqs = backward_last.shape[0]
    block_src = transition.shape[0]
    block_dst = transition.shape[1]
    seq_total = local_seqs * col_count
    forward_all = [None, lax.all_gather(forward[1], "col", axis=0, tiled=True)]
    columns = lax.broadcasted_iota(jnp.int32, (row_seqs, emission.shape[0]), 1)
    window = transition[:, :DW]
    totals = jnp.zeros((block_src, DW), jnp.float32)
    outputs = [None, None]
    beta = backward_last
    scale = jnp.full((seq_total, 1), 64.0, jnp.float32)
    chunk = block_src // CHUNKS
    for step in (1, 0):
        tokens = lax.dynamic_slice_in_dim(token_ids[step], row_index * row_seqs, row_seqs, 0)
        onehot = (tokens[:, None] == columns).astype(jnp.bfloat16)
        emitted = jnp.dot(onehot, emission, preferred_element_type=jnp.float32)
        local_back = (emitted * beta).astype(jnp.bfloat16)
        weighted_back = lax.all_gather(local_back, "row", axis=0, tiled=True)
        pieces = []
        norm = jnp.zeros((seq_total,), jnp.float32)
        mass = jnp.zeros((seq_total,), jnp.float32)
        if step == 0:
            forward_all[0] = lax.all_gather(forward[0], "col", axis=0, tiled=True)
        for k in range(CHUNKS):
            rows = slice(k * chunk, (k + 1) * chunk)
            partial = lax.dot_general(
                weighted_back, transition[rows], (((1,), (1,)), ((), ())), preferred_element_type=jnp.float32
            )
            norm = norm + jnp.sum(forward_all[step][:, rows].astype(jnp.float32) * partial, axis=1)
            mass = mass + jnp.sum(partial, axis=1)
            pieces.append(reduce_scatter(partial, scale, col_count, col_index, local_seqs))
        if step == 1:
            both = lax.psum(jnp.stack([norm, mass]), ("row", "col"))
            normal_all = both[0]
        else:
            normal_all = lax.psum(norm, ("row", "col"))
        normal_mine = lax.dynamic_slice_in_dim(normal_all, col_index * local_seqs, local_seqs, 0)
        scale_mine = lax.dynamic_slice_in_dim(scale, col_index * local_seqs, local_seqs, 0)
        mine = jnp.concatenate(pieces, axis=1) / (scale_mine * normal_mine[:, None])
        outputs[step] = mine
        if step == 1:
            halves = mine.reshape(local_seqs, ratio, block_dst)
            arrived = []
            for p in range(ratio):
                part = lax.dynamic_index_in_dim(halves, (col_index + p) % ratio, 1, keepdims=False)
                moves = []
                for r in range(row_count):
                    for c in range(col_count):
                        h = (c + p) % ratio
                        moves.append((r * col_count + c, (c // ratio) * col_count + r * ratio + h))
                arrived.append(lax.ppermute(part, ("row", "col"), moves))
            turned = jnp.stack([arrived[-i % ratio] for i in range(ratio)] * 2)
            start = (ratio - col_index % ratio) % ratio
            beta = lax.dynamic_slice_in_dim(turned, start, ratio, 0).reshape(row_seqs, block_dst)
            scale = (16777216.0 * both[0] / both[1])[:, None]
        scaled = (forward_all[step].astype(jnp.float32) / normal_all[:, None]).astype(jnp.bfloat16)
        totals = totals + lax.dot_general(
            scaled, weighted_back[:, :DW], (((0,), (0,)), ((), ())), preferred_element_type=jnp.float32
        )
    counts = window.astype(jnp.float32) * totals * (H * H / N)
    return (jnp.stack(outputs), counts)


def solution(mesh):
    in_specs = (P("row", "col"), P(None, "col"), P(), P(None, "col", "row"), P("row", "col"))
    out_specs = (P(None, "col", "row"), P("row", "col"))
    return jax.shard_map(
        on_device, mesh=mesh, in_specs=in_specs, out_specs=out_specs, check_vma=False
    )
```

```python
import jax
import jax.numpy as jnp
from jax import lax
from jax.sharding import PartitionSpec as P

H = 32768
N = 192
DW = 128
CHUNKS = 2


def in_order(arrived, index):
    count = len(arrived)
    turned = jnp.stack([arrived[-i % count] for i in range(count)] * 2)
    return lax.dynamic_slice_in_dim(turned, (count - index) % count, count, 0)


def gather_small(value, col_count, col_index):
    arrived = [value]
    for k in range(1, col_count):
        arrived.append(lax.ppermute(value, "col", [(c, (c + k) % col_count) for c in range(col_count)]))
    place = lax.broadcasted_iota(jnp.int32, (col_count,) + value.shape, 0)
    out = jnp.zeros(place.shape, value.dtype)
    for k, got in enumerate(arrived):
        out = jnp.where(place == (col_index - k + col_count) % col_count, got[None], out)
    return out


def gather_rows(value, row_count, row_index):
    half = row_count // 2
    arrived = [value]
    for k in range(1, half):
        arrived.append(lax.ppermute(value, "row", [(r, (r + 2 * k) % row_count) for r in range(row_count)]))
    own = in_order(arrived, row_index // 2) if half > 1 else value[None]
    got = lax.ppermute(own, "row", [(r, r ^ 1) for r in range(row_count)])
    even = row_index % 2 == 0
    both = jnp.stack([jnp.where(even, own, got), jnp.where(even, got, own)], axis=1)
    return both.reshape(row_count * value.shape[0], value.shape[1])


def split_pair(partial, scale, col_count, col_index, local_seqs):
    scaled = (partial * scale).reshape(col_count // 2, 2, local_seqs, partial.shape[1])
    side = col_index % 2
    away = lax.dynamic_index_in_dim(scaled, 1 - side, 1, keepdims=False).astype(jnp.float16)
    return away, lax.dynamic_index_in_dim(scaled, side, 1, keepdims=False)


def reduce_scatter(away, keep, col_count, col_index):
    half = col_count // 2
    got = lax.ppermute(away, "col", [(c, c ^ 1) for c in range(col_count)])
    pair = keep + got.astype(jnp.float32)
    here = col_index // 2
    total = lax.dynamic_index_in_dim(pair, here, 0, keepdims=False)
    packed = pair.astype(jnp.float16)
    for k in range(1, half):
        piece = lax.dynamic_index_in_dim(packed, (here + k) % half, 0, keepdims=False)
        got = lax.ppermute(piece, "col", [(c, (c + 2 * k) % col_count) for c in range(col_count)])
        total = total + got.astype(jnp.float32)
    return total


def on_device(transition, emission, token_ids, forward, backward_last):
    row_count = lax.axis_size("row")
    col_count = lax.axis_size("col")
    row_index = lax.axis_index("row")
    col_index = lax.axis_index("col")
    ratio = col_count // row_count
    local_seqs = forward.shape[1]
    row_seqs = backward_last.shape[0]
    block_src = transition.shape[0]
    block_dst = transition.shape[1]
    seq_total = local_seqs * col_count
    columns = lax.broadcasted_iota(jnp.int32, (row_seqs, emission.shape[0]), 1)
    window = transition[:, :DW]
    outputs = [None, None]
    normals = [None, None]
    picked = [None, None]
    beta = backward_last
    scale = jnp.full((seq_total, 1), 64.0, jnp.float32)
    scale_mine = jnp.full((local_seqs, 1), 64.0, jnp.float32)
    chunk = block_src // CHUNKS
    for step in (1, 0):
        tokens = lax.dynamic_slice_in_dim(token_ids[step], row_index * row_seqs, row_seqs, 0)
        onehot = (tokens[:, None] == columns).astype(jnp.bfloat16)
        emitted = jnp.dot(onehot, emission, preferred_element_type=jnp.float32)
        local_back = (emitted * beta).astype(jnp.bfloat16)
        weighted_back = gather_rows(local_back, row_count, row_index)
        picked[step] = weighted_back[:, :DW]
        if step == 1:
            forward_all = lax.all_gather(forward, "col", axis=1, tiled=True)
        pieces = []
        for k in range(CHUNKS):
            rows = slice(k * chunk, (k + 1) * chunk)
            partial = lax.dot_general(
                weighted_back, transition[rows], (((1,), (1,)), ((), ())), preferred_element_type=jnp.float32
            )
            away, keep = split_pair(partial, scale, col_count, col_index, local_seqs)
            if k < CHUNKS - 1:
                weighted_back, away = lax.optimization_barrier((weighted_back, away))
            pieces.append(reduce_scatter(away, keep, col_count, col_index))
        mine = jnp.concatenate(pieces, axis=1) / scale_mine
        norm = jnp.sum(forward[step].astype(jnp.float32) * mine, axis=1)
        sums = lax.psum(jnp.stack([norm, jnp.sum(mine, axis=1)]), "row")
        sums_all = gather_small(sums, col_count, col_index)
        normals[step] = sums_all[:, 0].reshape(seq_total)
        outputs[step] = mine / sums[0][:, None]
        if step == 1:
            halves = outputs[step].reshape(local_seqs, ratio, block_dst)
            arrived = []
            for p in range(ratio):
                part = lax.dynamic_index_in_dim(halves, (col_index + p) % ratio, 1, keepdims=False)
                moves = []
                for r in range(row_count):
                    for c in range(col_count):
                        moves.append((r * col_count + c, (c // ratio) * col_count + r * ratio + (c + p) % ratio))
                arrived.append(lax.ppermute(part, ("row", "col"), moves))
            beta = in_order(arrived, col_index % ratio).reshape(row_seqs, block_dst)
            scale = (16777216.0 * sums_all[:, 0] / sums_all[:, 1]).reshape(seq_total, 1)
            scale_mine = (16777216.0 * sums[0] / sums[1])[:, None]
    totals = jnp.zeros((block_src, DW), jnp.float32)
    for step in (1, 0):
        scaled = (forward_all[step].astype(jnp.float32) / normals[step][:, None]).astype(jnp.bfloat16)
        totals = totals + lax.dot_general(
            scaled, picked[step], (((0,), (0,)), ((), ())), preferred_element_type=jnp.float32
        )
    counts = window.astype(jnp.float32) * totals * (H * H / N)
    return (jnp.stack(outputs), counts)


def solution(mesh):
    in_specs = (P("row", "col"), P(None, "col"), P(), P(None, "col", "row"), P("row", "col"))
    out_specs = (P(None, "col", "row"), P("row", "col"))
    return jax.shard_map(
        on_device, mesh=mesh, in_specs=in_specs, out_specs=out_specs, check_vma=False
    )
```

```python
import jax
import jax.numpy as jnp
from jax import lax
from jax.sharding import PartitionSpec as P

H = 32768
N = 192
DW = 128
CHUNKS = 2


def in_order(arrived, index):
    count = len(arrived)
    turned = jnp.stack([arrived[-i % count] for i in range(count)] * 2)
    return lax.dynamic_slice_in_dim(turned, (count - index) % count, count, 0)


def gather_small(value, col_count, col_index):
    block = value[None]
    while block.shape[0] < col_count:
        step = block.shape[0]
        got = lax.ppermute(block, "col", [(c, c ^ step) for c in range(col_count)])
        first = col_index // step % 2 == 0
        block = jnp.where(first, jnp.concatenate([block, got]), jnp.concatenate([got, block]))
    return block


def gather_rows(value, row_count, row_index):
    half = row_count // 2
    arrived = [value]
    for k in range(1, half):
        arrived.append(lax.ppermute(value, "row", [(r, (r + 2 * k) % row_count) for r in range(row_count)]))
    own = in_order(arrived, row_index // 2) if half > 1 else value[None]
    got = lax.ppermute(own, "row", [(r, r ^ 1) for r in range(row_count)])
    even = row_index % 2 == 0
    both = jnp.stack([jnp.where(even, own, got), jnp.where(even, got, own)], axis=1)
    return both.reshape(row_count * value.shape[0], value.shape[1])


def split_pair(partial, scale, col_count, col_index, local_seqs):
    scaled = (partial * scale).reshape(col_count // 2, 2, local_seqs, partial.shape[1])
    side = col_index % 2
    away = lax.dynamic_index_in_dim(scaled, 1 - side, 1, keepdims=False).astype(jnp.float16)
    return away, lax.dynamic_index_in_dim(scaled, side, 1, keepdims=False)


def reduce_scatter(away, keep, col_count, col_index):
    half = col_count // 2
    got = lax.ppermute(away, "col", [(c, c ^ 1) for c in range(col_count)])
    pair = keep + got.astype(jnp.float32)
    here = col_index // 2
    total = lax.dynamic_index_in_dim(pair, here, 0, keepdims=False)
    packed = pair.astype(jnp.float16)
    for k in range(1, half):
        piece = lax.dynamic_index_in_dim(packed, (here + k) % half, 0, keepdims=False)
        got = lax.ppermute(piece, "col", [(c, (c + 2 * k) % col_count) for c in range(col_count)])
        total = total + got.astype(jnp.float32)
    return total


def on_device(transition, emission, token_ids, forward, backward_last):
    row_count = lax.axis_size("row")
    col_count = lax.axis_size("col")
    row_index = lax.axis_index("row")
    col_index = lax.axis_index("col")
    ratio = col_count // row_count
    local_seqs = forward.shape[1]
    row_seqs = backward_last.shape[0]
    block_src = transition.shape[0]
    block_dst = transition.shape[1]
    seq_total = local_seqs * col_count
    columns = lax.broadcasted_iota(jnp.int32, (row_seqs, emission.shape[0]), 1)
    window = transition[:, :DW]
    outputs = [None, None]
    normals = [None, None]
    picked = [None, None]
    beta = backward_last
    scale = jnp.full((seq_total, 1), 64.0, jnp.float32)
    scale_mine = jnp.full((local_seqs, 1), 64.0, jnp.float32)
    chunk = block_src // CHUNKS
    for step in (1, 0):
        tokens = lax.dynamic_slice_in_dim(token_ids[step], row_index * row_seqs, row_seqs, 0)
        onehot = (tokens[:, None] == columns).astype(jnp.bfloat16)
        emitted = jnp.dot(onehot, emission, preferred_element_type=jnp.float32)
        local_back = (emitted * beta).astype(jnp.bfloat16)
        weighted_back = gather_rows(local_back, row_count, row_index)
        picked[step] = weighted_back[:, :DW]
        if step == 1:
            forward_all = lax.all_gather(forward, "col", axis=1, tiled=True)
        pieces = []
        for k in range(CHUNKS):
            rows = slice(k * chunk, (k + 1) * chunk)
            partial = lax.dot_general(
                weighted_back, transition[rows], (((1,), (1,)), ((), ())), preferred_element_type=jnp.float32
            )
            away, keep = split_pair(partial, scale, col_count, col_index, local_seqs)
            if k < CHUNKS - 1:
                weighted_back, away = lax.optimization_barrier((weighted_back, away))
            pieces.append(reduce_scatter(away, keep, col_count, col_index))
        mine = jnp.concatenate(pieces, axis=1) / scale_mine
        norm = jnp.sum(forward[step].astype(jnp.float32) * mine, axis=1)
        sums = lax.psum(jnp.stack([norm, jnp.sum(mine, axis=1)]), "row")
        outputs[step] = mine / sums[0][:, None]
        if step == 1:
            halves = outputs[step].reshape(local_seqs, ratio, block_dst)
            arrived = []
            for p in range(ratio):
                part = lax.dynamic_index_in_dim(halves, (col_index + p) % ratio, 1, keepdims=False)
                moves = []
                for r in range(row_count):
                    for c in range(col_count):
                        moves.append((r * col_count + c, (c // ratio) * col_count + r * ratio + (c + p) % ratio))
                arrived.append(lax.ppermute(part, ("row", "col"), moves))
            beta = in_order(arrived, col_index % ratio).reshape(row_seqs, block_dst)
            beta, sums = lax.optimization_barrier((beta, sums))
            sums_all = gather_small(sums, col_count, col_index)
            normals[step] = sums_all[:, 0].reshape(seq_total)
            scale = (16777216.0 * sums_all[:, 0] / sums_all[:, 1]).reshape(seq_total, 1)
            scale_mine = (16777216.0 * sums[0] / sums[1])[:, None]
    normals[0] = gather_small(sums, col_count, col_index)[:, 0].reshape(seq_total)
    totals = jnp.zeros((block_src, DW), jnp.float32)
    for step in (1, 0):
        scaled = (forward_all[step].astype(jnp.float32) / normals[step][:, None]).astype(jnp.bfloat16)
        totals = totals + lax.dot_general(
            scaled, picked[step], (((0,), (0,)), ((), ())), preferred_element_type=jnp.float32
        )
    counts = window.astype(jnp.float32) * totals * (H * H / N)
    return (jnp.stack(outputs), counts)


def solution(mesh):
    in_specs = (P("row", "col"), P(None, "col"), P(), P(None, "col", "row"), P("row", "col"))
    out_specs = (P(None, "col", "row"), P("row", "col"))
    return jax.shard_map(
        on_device, mesh=mesh, in_specs=in_specs, out_specs=out_specs, check_vma=False
    )
```
